32 devices in a mesh: wall: 4 (over x, core), surf: 8 (over z, y).
Axes of the slice: x: 2, y: 2, z: 4, core: 2. Of those that a mesh axis runs over, the one named last changes fastest.
Arguments:
- primal: bfloat16 [6, 128, 8192], P(None, 'wall', 'surf'), may hold values from -6 to 6
- adjoint: bfloat16 [6, 128, 8192], P(None, 'wall', 'surf'), may hold values from -6 to 6
- coords: float32 [3, 128, 8192], P(None, 'wall', 'surf'), may hold values from -6 to 6
- foot_index: int32 [2, 128, 8192], P(None, 'wall', 'surf'), may hold values from 0 to 15
- foot_weight: float32 [2, 128, 8192], P(None, 'wall', 'surf'), may hold values from 0.002 to 0.02
- blanking: int32 [128, 8192], P('wall', 'surf'), may hold values 0 or 1
- owner_map: int32 [8192], replicated, may hold values from 0 to 8191, as said below
Outputs:
- surface_sens: float32 [3, 8192], P(None, 'surf')
The draws below stay inside these ranges and needn't reach their ends.
Inputs may be any that keep to these rules, and one draw needn't show every extreme that they name: `owner_map`: each control point is named by exactly one output slot; slot c * 1024 + b * 128 + i, for i below 128, names a control point of the aligned block b of 1024 control points. `foot_index`: offsets of control points from a grid point's column, plus 8.
All inputs are finite; a program needn't handle non-finite values. No bound on the sum of `blanking` on one device may be relied on, other than what follows from the above.
Results may differ from the reference program's by a relative error of at most 0.0003.
Values may be sent and summed in bfloat16 or wider, within the bound.
A program may use at most 128 MiB of HBM per device.

```python
import math
import jax
import jax.numpy as jnp
from jax import lax

SDEV = 1024
NVAR = 6
NL = 128
NS = 8192
N_SURF = 8


def draw_owner_map(key, part):
    key = jax.random.fold_in(key, 11)
    share = SDEV // N_SURF
    block_keys = jax.random.split(key, N_SURF)
    orders = jax.vmap(lambda k: jax.random.permutation(k, SDEV))(block_keys).astype(jnp.int32)
    source_block = jnp.arange(N_SURF, dtype=jnp.int32)[:, None, None]
    points = source_block * SDEV + orders.reshape(N_SURF, N_SURF, share)
    return jnp.transpose(points, (1, 0, 2)).reshape(-1).astype(jnp.int32)


def touch_ends(entries, key, smallest, largest):
    place = [jax.random.randint(jax.random.fold_in(key, axis), (), 0, length) for axis, length in enumerate(entries.shape)]
    longest = entries.shape.index(max(entries.shape))
    beside = place[:longest] + [(place[longest] + 1) % entries.shape[longest]] + place[longest + 1:]
    return entries.at[tuple(place)].set(smallest).at[tuple(beside)].set(largest)


def block_levels(stream_key, dims, pieces, smallest, high):
    def one(position, shards_of):
        draws = jax.random.uniform(jax.random.fold_in(jax.random.fold_in(stream_key, 6), position), (shards_of,), jnp.float32, smallest / len(pieces), high / len(pieces))
        return jnp.repeat(jnp.exp(draws), dims[position] // shards_of).reshape((-1,) + (1,) * (len(dims) - position - 1))

    level = one(*pieces[0])
    for cut in pieces[1:]:
        level = level * one(*cut)
    return level


def bell_draw(key, shape, scale, limit, pieces=(), kind=jnp.bfloat16):
    drawn = scale * jax.random.normal(key, shape, jnp.float32)
    if pieces:
        drawn = drawn * block_levels(key, shape, pieces, -0.22, 0.18)
    return jnp.clip(drawn, -limit, limit).astype(kind)


def setup_inputs(seed: int = 0) -> dict:
    seeds = jax.random.split(jax.random.key(seed), 8)
    return {
        "primal": bell_draw(seeds[0], (NVAR, NL, NS), 1.0, 6.0, ((1, 4), (2, 8))),
        "adjoint": bell_draw(seeds[1], (NVAR, NL, NS), 1.0, 6.0, ((1, 4), (2, 8))),
        "coords": bell_draw(seeds[2], (3, NL, NS), 1.0, 6.0, ((1, 4), (2, 8)), jnp.float32),
        "foot_index": touch_ends(jax.random.randint(seeds[3], (2, NL, NS), 0, 16), jax.random.fold_in(seeds[3], 1), 0, 15).astype(jnp.int32),
        "foot_weight": jnp.clip(jnp.exp(math.log(0.02) - 2.30258502 * jax.random.uniform(seeds[4], (2, NL, NS), jnp.float32) ** block_levels(seeds[4], (2, NL, NS), ((1, 4), (2, 8)), -0.2, 0.2)), 0.002, 0.02),
        "blanking": touch_ends((jax.random.randint(seeds[5], (NL, NS), 0, 8) < 7).astype(jnp.int32), jax.random.fold_in(seeds[5], 1), 0, 1),
        "owner_map": draw_owner_map(jax.random.fold_in(seeds[7], 71), 0),
    }


def face_term(q_low, q_high, a_low, a_high, x_low, x_high):
    average = 0.5 * (q_low + q_high)
    jump = q_high - q_low
    adjoint_jump = a_low - a_high
    face_normal = x_high - x_low
    along_sum = jnp.sum(adjoint_jump * average, axis=0)
    across_sum = jnp.sum(adjoint_jump * jump, axis=0)
    return along_sum * average[1:4] + average[4] * adjoint_jump[1:4] - across_sum * face_normal


def reference(primal, adjoint, coords, foot_index, foot_weight, blanking, owner_map):
    layer_total = primal.shape[1]
    column_total = primal.shape[2]
    fields = jnp.concatenate([primal, adjoint], axis=0)
    padded_fields = jnp.pad(fields, ((0, 0), (1, 1), (1, 1)))
    padded_coords = jnp.pad(coords, ((0, 0), (1, 1), (1, 1)))
    column_ids = jnp.arange(column_total, dtype=jnp.int32)

    def layer_step(accumulated, layer_index):
        three_rows = lax.dynamic_slice_in_dim(padded_fields, layer_index, 3, 1).astype(jnp.float32)
        three_coords = lax.dynamic_slice_in_dim(padded_coords, layer_index, 3, 1)
        q_cols = three_rows[:6, :, 1:-1]
        a_cols = three_rows[6:, :, 1:-1]
        x_cols = three_coords[:, :, 1:-1]
        wall_h = face_term(q_cols[:, :-1], q_cols[:, 1:], a_cols[:, :-1], a_cols[:, 1:], x_cols[:, :-1], x_cols[:, 1:])
        sensitivity = wall_h[:, 0] - wall_h[:, 1]
        q_row = three_rows[:6, 1]
        a_row = three_rows[6:, 1]
        x_row = three_coords[:, 1]
        surf_h = face_term(q_row[:, :-1], q_row[:, 1:], a_row[:, :-1], a_row[:, 1:], x_row[:, :-1], x_row[:, 1:])
        sensitivity = sensitivity + surf_h[:, :-1] - surf_h[:, 1:]
        alive_mask = lax.dynamic_index_in_dim(blanking, layer_index, 0, keepdims=False).astype(jnp.float32)
        for entry in range(2):
            offset_row = lax.dynamic_index_in_dim(foot_index[entry], layer_index, 0, keepdims=False)
            weight_row = lax.dynamic_index_in_dim(foot_weight[entry], layer_index, 0, keepdims=False)
            point_row = jnp.mod(column_ids + offset_row - 8, column_total).astype(jnp.int32)
            accumulated = accumulated.at[:, point_row].add((alive_mask * weight_row) * sensitivity)
        return accumulated, None

    start_sum = jnp.zeros((3, column_total), jnp.float32)
    point_sum, unused = lax.scan(layer_step, start_sum, jnp.arange(layer_total, dtype=jnp.int32))
    return point_sum[:, owner_map.astype(jnp.int32)]
```

```python
import functools

import jax
import jax.numpy as jnp
from jax import lax
from jax.experimental import pallas as pl
from jax.experimental.pallas import tpu as pltpu
from jax.sharding import PartitionSpec as P

LANES = 128
NV = 15


def face(low, high):
    jumps = [low[6 + v] - high[6 + v] for v in range(6)]
    sums = [low[v] + high[v] for v in range(6)]
    along = sum(jumps[v] * sums[v] for v in range(6)) * 0.25
    across = sum(jumps[v] * (high[v] - low[v]) for v in range(6))
    half = 0.5 * sums[4]
    return [
        along * sums[1 + k] + half * jumps[1 + k] - across * (high[12 + k] - low[12 + k])
        for k in range(3)
    ]


def fold(tiles, sub):
    for bit in (1, 2, 4):
        clear = (sub & bit) == 0
        folded = []
        for a, b in zip(tiles[0::2], tiles[1::2]):
            folded.append(jnp.where(clear, a, b) + pltpu.roll(jnp.where(clear, b, a), bit, 0))
        tiles = folded
    return tiles[0]


def kernel(
    n_wall,
    n_surf,
    primal,
    adjoint,
    coords,
    foot_index,
    foot_weight,
    blanking,
    owner,
    out,
    q_in,
    a_in,
    x_in,
    index_in,
    weight_in,
    blank_in,
    owner_in,
    field,
    before,
    row_low,
    row_high,
    col_low,
    col_high,
    from_below,
    from_above,
    from_left,
    from_right,
    wall_h,
    surf_h,
    window,
    packet,
    arrived,
    partial,
    load_sem,
    halo_send,
    halo_recv,
    slot_send,
    slot_recv,
    wall_send,
    wall_recv,
):
    layers, columns = blank_in.shape
    chunks = columns // LANES
    groups = layers // 8
    w = lax.axis_index("wall")
    s = lax.axis_index("surf")

    loads = [
        pltpu.make_async_copy(src, dst, load_sem.at[i])
        for i, (src, dst) in enumerate(
            (
                (primal, q_in),
                (adjoint, a_in),
                (coords, x_in),
                (foot_index, index_in),
                (foot_weight, weight_in),
                (blanking, blank_in),
                (owner, owner_in),
            )
        )
    ]
    for load in loads:
        load.start()

    barrier = pltpu.get_barrier_semaphore()
    for step in range(1, n_wall):
        peer = lax.rem(w + step, n_wall)
        pl.semaphore_signal(barrier, inc=1, device_id=(peer, s), device_id_type=pl.DeviceIdType.MESH)
    for step in range(1, n_surf):
        peer = lax.rem(s + step, n_surf)
        pl.semaphore_signal(barrier, inc=1, device_id=(w, peer), device_id_type=pl.DeviceIdType.MESH)

    lane32 = lax.broadcasted_iota(jnp.int32, (layers, LANES), 1)
    lane = lax.broadcasted_iota(jnp.int32, (8, LANES), 1)
    sub = lax.broadcasted_iota(jnp.int32, (8, LANES), 0)

    t_low = jnp.zeros((layers, LANES), jnp.float32)
    t_high = jnp.zeros((layers, LANES), jnp.float32)
    for v in range(NV):
        if v in (0, 6, 12):
            loads[v // 6].wait()
        source = (q_in, a_in, x_in)[v // 6]
        previous = None
        for c in range(chunks):
            x = source[v % 6, :, c * LANES : (c + 1) * LANES].astype(jnp.float32)
            field[v, c, 8 : 8 + layers, :] = x
            row_low[v, c : c + 1, :] = x[0:1]
            row_high[v, c : c + 1, :] = x[layers - 1 : layers]
            rolled = pltpu.roll(x, 1, 1)
            before[v, c] = rolled if c == 0 else jnp.where(lane32 == 0, previous, rolled)
            previous = rolled
            if c == 0:
                t_low = jnp.where(lane32 == v, jnp.broadcast_to(x[:, 0:1], x.shape), t_low)
            if c == chunks - 1:
                t_high = jnp.where(
                    lane32 == v, jnp.broadcast_to(x[:, LANES - 1 : LANES], x.shape), t_high
                )
    col_low[...] = t_low
    col_high[...] = t_high

    pl.semaphore_wait(barrier, n_wall + n_surf - 2)

    def halo(number, src, dst, target):
        return pltpu.make_async_remote_copy(
            src_ref=src,
            dst_ref=dst,
            send_sem=halo_send.at[number],
            recv_sem=halo_recv.at[number],
            device_id=target,
            device_id_type=pl.DeviceIdType.MESH,
        )

    to_above = halo(0, row_high, from_below, (lax.rem(w + 1, n_wall), s))
    to_below = halo(1, row_low, from_above, (lax.rem(w + n_wall - 1, n_wall), s))
    to_right = halo(2, col_high, from_left, (w, lax.rem(s + 1, n_surf)))
    to_left = halo(3, col_low, from_right, (w, lax.rem(s + n_surf - 1, n_surf)))
    sends = (
        (to_above, w < n_wall - 1),
        (to_below, w > 0),
        (to_right, s < n_surf - 1),
        (to_left, s > 0),
    )
    receives = (
        (to_above, w > 0, from_below),
        (to_below, w < n_wall - 1, from_above),
        (to_right, s > 0, from_left),
        (to_left, s < n_surf - 1, from_right),
    )
    for copy, wanted in sends:
        pl.when(wanted)(copy.start)

    def interior(c, carry):
        for g in range(groups):
            rows = pl.ds(8 + 8 * g, 8)
            high = [field[v, c, rows, :] for v in range(NV)]
            low = [field[v, c, pl.ds(7 + 8 * g, 8), :] for v in range(NV)]
            for k, h in enumerate(face(low, high)):
                wall_h[k, c, pl.ds(8 * g, 8), :] = h
            low = [before[v, c, pl.ds(8 * g, 8), :] for v in range(NV)]
            for k, h in enumerate(face(low, high)):
                surf_h[k, c, pl.ds(8 * g, 8), :] = h
        return carry

    for v in range(NV):
        field[v, :, 0:8, :] = jnp.zeros((chunks, 8, LANES), jnp.float32)
    lax.fori_loop(0, chunks, interior, 0)
    window[...] = jnp.zeros_like(window)

    for copy, wanted, landing in receives:
        pl.when(wanted)(copy.wait_recv)

        @pl.when(jnp.logical_not(wanted))
        def _():
            landing[...] = jnp.zeros_like(landing)

    below = face([from_below[v] for v in range(NV)], [row_low[v] for v in range(NV)])
    above = face([row_high[v] for v in range(NV)], [from_above[v] for v in range(NV)])
    for k in range(3):
        for c in range(chunks):
            wall_h[k, c, 0:1, :] = below[k][c : c + 1]
            wall_h[k, c, layers : layers + 1, :] = above[k][c : c + 1]
    for g in range(groups):
        rows = pl.ds(8 * g, 8)
        left = from_left[rows, :]
        right = from_right[rows, :]
        left = [jnp.broadcast_to(left[:, v : v + 1], (8, LANES)) for v in range(NV)]
        right = [jnp.broadcast_to(right[:, v : v + 1], (8, LANES)) for v in range(NV)]
        inner = pl.ds(8 + 8 * g, 8)
        first = face(left, [field[v, 0, inner, :] for v in range(NV)])
        last = face([field[v, chunks - 1, inner, :] for v in range(NV)], right)
        for k in range(3):
            surf_h[k, 0, rows, :] = jnp.where(lane == 0, first[k], surf_h[k, 0, rows, :])
            surf_h[k, chunks, rows, :] = pltpu.roll(last[k], 1, 1)

    for load in loads[3:]:
        load.wait()

    def gather_points(c, carry):
        span = pl.ds(pl.multiple_of(c * LANES, LANES), LANES)
        sens, index, weight = [], [], []
        for g in range(groups):
            rows = pl.ds(8 * g, 8)
            live = blank_in[rows, span].astype(jnp.float32)
            index.append([index_in[t, rows, span] for t in range(2)])
            weight.append([live * weight_in[t, rows, span] for t in range(2)])
            sens.append(
                [
                    wall_h[k, c, rows, :]
                    - wall_h[k, c, pl.ds(8 * g + 1, 8), :]
                    + surf_h[k, c, rows, :]
                    - jnp.where(
                        lane == LANES - 1,
                        pltpu.roll(surf_h[k, c + 1, rows, :], LANES - 1, 1),
                        pltpu.roll(surf_h[k, c, rows, :], LANES - 1, 1),
                    )
                    for k in range(3)
                ]
            )
        sums = [[], [], []]
        for offset in range(16):
            total = [None] * 3
            for g in range(groups):
                picked = jnp.where(index[g][0] == offset, weight[g][0], 0.0) + jnp.where(
                    index[g][1] == offset, weight[g][1], 0.0
                )
                for k in range(3):
                    term = picked * sens[g][k]
                    total[k] = term if total[k] is None else total[k] + term
            for k in range(3):
                sums[k].append(total[k])
        for k in range(3):
            down = pltpu.roll(fold(sums[k][:8], sub), LANES - 8, 1, stride=1, stride_axis=0)
            up = pltpu.roll(fold(sums[k][8:], sub), 0, 1, stride=1, stride_axis=0)
            to_left = lane >= LANES - 8 + sub
            to_right = lane < sub
            window[k, c] += jnp.where(to_left, down, 0.0)
            window[k, c + 1] += jnp.where(to_left, 0.0, down) + jnp.where(to_right, 0.0, up)
            window[k, c + 2] += jnp.where(to_right, up, 0.0)
        return carry

    lax.fori_loop(0, chunks, gather_points, 0)

    points = [fold([window[k, c + 1] for c in range(chunks)], sub) for k in range(3)]
    over = [jnp.sum(window[k, 0] + window[k, chunks + 1], axis=0, keepdims=True) for k in range(3)]

    for r in range(n_surf // 8):
        local = owner_in[pl.ds(s + 8 * r * n_surf, 8, stride=n_surf), :] - s * columns
        place = local & (LANES - 1)
        chunk = local >> 7
        for k in range(3):
            value = jnp.zeros((8, LANES), jnp.float32)
            for c in range(chunks):
                row = jnp.broadcast_to(points[k][c : c + 1], (8, LANES))
                value = jnp.where(chunk == c, jnp.take_along_axis(row, place, axis=1), value)
            packet[pl.ds(64 * r + k, 8, stride=8), :] = value
            packet[pl.ds(64 * r + 3 + k, 8, stride=8), :] = jnp.broadcast_to(over[k], (8, LANES))

    def slot_copy(target, source):
        return pltpu.make_async_remote_copy(
            src_ref=packet.at[pl.ds(pl.multiple_of(target * 8, 8), 8), :],
            dst_ref=arrived.at[pl.ds(pl.multiple_of(source * 8, 8), 8), :],
            send_sem=slot_send.at[target],
            recv_sem=slot_recv.at[source],
            device_id=(w, target),
            device_id_type=pl.DeviceIdType.MESH,
        )

    peers = [lax.rem(s + step, n_surf) for step in range(1, n_surf)]
    for peer in peers:
        slot_copy(peer, s).start()
    mine = pl.ds(pl.multiple_of(s * 8, 8), 8)
    arrived[mine, :] = packet[mine, :]
    for peer in peers:
        slot_copy(peer, peer).wait_recv()

    parts = partial.at[w]
    over = [arrived[pl.ds(3 + k, n_surf, stride=8), :] for k in range(3)]
    for k in range(3):
        ahead = jnp.concatenate([over[k][n_surf - 1 :], over[k][: n_surf - 1]], axis=0)
        behind = jnp.concatenate([over[k][1:], over[k][:1]], axis=0)
        for r in range(n_surf // 8):
            block = sub + 8 * r
            local = owner_in[pl.ds(pl.multiple_of(s * n_surf, 8) + 8 * r, 8), :] - block * columns
            place = local & (LANES - 1)
            value = arrived[pl.ds(64 * r + k, 8, stride=8), :]
            first = jnp.take_along_axis(ahead[8 * r : 8 * r + 8], place, axis=1)
            last = jnp.take_along_axis(behind[8 * r : 8 * r + 8], place, axis=1)
            value = value + jnp.where(local < 8, first, 0.0)
            value = value + jnp.where(local >= columns - 8, last, 0.0)
            parts[k, 8 * r : 8 * r + 8, :] = value

    def wall_copy(target, source):
        return pltpu.make_async_remote_copy(
            src_ref=partial.at[w],
            dst_ref=partial.at[source],
            send_sem=wall_send.at[target],
            recv_sem=wall_recv.at[source],
            device_id=(target, s),
            device_id_type=pl.DeviceIdType.MESH,
        )

    walls = [lax.rem(w + step, n_wall) for step in range(1, n_wall)]
    for peer in walls:
        wall_copy(peer, w).start()
    for copy, wanted in sends:
        pl.when(wanted)(copy.wait_send)
    for peer in peers:
        slot_copy(peer, s).wait_send()
    for peer in walls:
        wall_copy(peer, peer).wait_recv()
    total = partial[0]
    for other in range(1, n_wall):
        total = total + partial[other]
    out[...] = total
    for peer in walls:
        wall_copy(peer, w).wait_send()


def body(primal, adjoint, coords, foot_index, foot_weight, blanking, owner_map):
    n_wall = lax.axis_size("wall")
    n_surf = lax.axis_size("surf")
    layers, columns = blanking.shape
    chunks = columns // LANES
    share = columns // n_surf
    owner = owner_map.reshape(n_surf * n_surf, share)
    if share < LANES:
        owner = jnp.pad(owner, ((0, 0), (0, LANES - share)))
    f32 = jnp.float32
    scratch = [
        pltpu.VMEM(primal.shape, primal.dtype),
        pltpu.VMEM(adjoint.shape, adjoint.dtype),
        pltpu.VMEM(coords.shape, coords.dtype),
        pltpu.VMEM(foot_index.shape, jnp.int32),
        pltpu.VMEM(foot_weight.shape, f32),
        pltpu.VMEM(blanking.shape, jnp.int32),
        pltpu.VMEM(owner.shape, jnp.int32),
        pltpu.VMEM((NV, chunks, layers + 8, LANES), f32),
        pltpu.VMEM((NV, chunks, layers, LANES), f32),
        pltpu.VMEM((NV, chunks, LANES), f32),
        pltpu.VMEM((NV, chunks, LANES), f32),
        pltpu.VMEM((layers, LANES), f32),
        pltpu.VMEM((layers, LANES), f32),
        pltpu.VMEM((NV, chunks, LANES), f32),
        pltpu.VMEM((NV, chunks, LANES), f32),
        pltpu.VMEM((layers, LANES), f32),
        pltpu.VMEM((layers, LANES), f32),
        pltpu.VMEM((3, chunks, layers + 8, LANES), f32),
        pltpu.VMEM((3, chunks + 1, layers, LANES), f32),
        pltpu.VMEM((3, chunks + 2, 8, LANES), f32),
        pltpu.VMEM((n_surf * 8, LANES), f32),
        pltpu.VMEM((n_surf * 8, LANES), f32),
        pltpu.VMEM((n_wall, 3, n_surf, LANES), f32),
        pltpu.SemaphoreType.DMA((7,)),
        pltpu.SemaphoreType.DMA((4,)),
        pltpu.SemaphoreType.DMA((4,)),
        pltpu.SemaphoreType.DMA((n_surf,)),
        pltpu.SemaphoreType.DMA((n_surf,)),
        pltpu.SemaphoreType.DMA((n_wall,)),
        pltpu.SemaphoreType.DMA((n_wall,)),
    ]
    summed = pl.pallas_call(
        functools.partial(kernel, n_wall, n_surf),
        out_shape=jax.ShapeDtypeStruct((3, n_surf, LANES), f32),
        in_specs=[pl.BlockSpec(memory_space=pl.ANY)] * 7,
        out_specs=pl.BlockSpec(memory_space=pltpu.VMEM),
        scratch_shapes=scratch,
        compiler_params=pltpu.CompilerParams(
            collective_id=0, has_side_effects=True, vmem_limit_bytes=32 * 1024 * 1024
        ),
    )(primal, adjoint, coords, foot_index, foot_weight, blanking, owner)
    return summed[:, :, :share].reshape(3, columns)


def solution(mesh):
    placed = (
        P(None, "wall", "surf"),
        P(None, "wall", "surf"),
        P(None, "wall", "surf"),
        P(None, "wall", "surf"),
        P(None, "wall", "surf"),
        P("wall", "surf"),
        P(),
    )
    return jax.shard_map(
        body, mesh=mesh, in_specs=placed, out_specs=P(None, "surf"), check_vma=False
    )
```

```python
import functools

import jax
import jax.numpy as jnp
from jax import lax
from jax.experimental import pallas as pl
from jax.experimental.pallas import tpu as pltpu
from jax.sharding import PartitionSpec as P

LANES = 128
NV = 15


def face(low, high):
    jumps = [low[6 + v] - high[6 + v] for v in range(6)]
    sums = [low[v] + high[v] for v in range(6)]
    along = sum(jumps[v] * sums[v] for v in range(6)) * 0.25
    across = sum(jumps[v] * (high[v] - low[v]) for v in range(6))
    half = 0.5 * sums[4]
    return [
        along * sums[1 + k] + half * jumps[1 + k] - across * (high[12 + k] - low[12 + k])
        for k in range(3)
    ]


def fold(tiles, sub):
    for bit in (1, 2, 4):
        clear = (sub & bit) == 0
        folded = []
        for a, b in zip(tiles[0::2], tiles[1::2]):
            folded.append(jnp.where(clear, a, b) + pltpu.roll(jnp.where(clear, b, a), bit, 0))
        tiles = folded
    return tiles[0]


def kernel(
    n_wall,
    n_surf,
    primal,
    adjoint,
    coords,
    foot_index,
    foot_weight,
    blanking,
    owner,
    out,
    q_in,
    a_in,
    x_in,
    index_in,
    weight_in,
    blank_in,
    owner_in,
    field,
    before,
    row_low,
    row_high,
    col_low,
    col_high,
    from_below,
    from_above,
    from_left,
    from_right,
    wall_h,
    surf_h,
    window,
    packet,
    arrived,
    load_sem,
    halo_send,
    halo_recv,
    slot_send,
    slot_recv,
):
    layers, columns = blank_in.shape
    chunks = columns // LANES
    groups = layers // 8
    w = lax.axis_index("wall")
    s = lax.axis_index("surf")

    loads = [
        pltpu.make_async_copy(src, dst, load_sem.at[i])
        for i, (src, dst) in enumerate(
            (
                (primal, q_in),
                (adjoint, a_in),
                (coords, x_in),
                (foot_index, index_in),
                (foot_weight, weight_in),
                (blanking, blank_in),
                (owner, owner_in),
            )
        )
    ]
    for load in loads:
        load.start()

    barrier = pltpu.get_barrier_semaphore()
    peers = [
        (lax.rem(w + up, n_wall), lax.rem(s + along, n_surf))
        for along in range(n_surf)
        for up in range(n_wall)
        if up or along
    ]
    for peer in peers:
        pl.semaphore_signal(barrier, inc=1, device_id=peer, device_id_type=pl.DeviceIdType.MESH)

    lane32 = lax.broadcasted_iota(jnp.int32, (layers, LANES), 1)
    lane = lax.broadcasted_iota(jnp.int32, (8, LANES), 1)
    sub = lax.broadcasted_iota(jnp.int32, (8, LANES), 0)

    t_low = jnp.zeros((layers, LANES), jnp.float32)
    t_high = jnp.zeros((layers, LANES), jnp.float32)
    for v in range(NV):
        if v in (0, 6, 12):
            loads[v // 6].wait()
        source = (q_in, a_in, x_in)[v // 6]
        previous = None
        for c in range(chunks):
            x = source[v % 6, :, c * LANES : (c + 1) * LANES].astype(jnp.float32)
            field[v, c, 8 : 8 + layers, :] = x
            row_low[v, c : c + 1, :] = x[0:1]
            row_high[v, c : c + 1, :] = x[layers - 1 : layers]
            rolled = pltpu.roll(x, 1, 1)
            before[v, c] = rolled if c == 0 else jnp.where(lane32 == 0, previous, rolled)
            previous = rolled
            if c == 0:
                t_low = jnp.where(lane32 == v, jnp.broadcast_to(x[:, 0:1], x.shape), t_low)
            if c == chunks - 1:
                t_high = jnp.where(
                    lane32 == v, jnp.broadcast_to(x[:, LANES - 1 : LANES], x.shape), t_high
                )
    col_low[...] = t_low
    col_high[...] = t_high

    pl.semaphore_wait(barrier, len(peers))

    def halo(number, src, dst, target):
        return pltpu.make_async_remote_copy(
            src_ref=src,
            dst_ref=dst,
            send_sem=halo_send.at[number],
            recv_sem=halo_recv.at[number],
            device_id=target,
            device_id_type=pl.DeviceIdType.MESH,
        )

    to_above = halo(0, row_high, from_below, (lax.rem(w + 1, n_wall), s))
    to_below = halo(1, row_low, from_above, (lax.rem(w + n_wall - 1, n_wall), s))
    to_right = halo(2, col_high, from_left, (w, lax.rem(s + 1, n_surf)))
    to_left = halo(3, col_low, from_right, (w, lax.rem(s + n_surf - 1, n_surf)))
    sends = (
        (to_above, w < n_wall - 1),
        (to_below, w > 0),
        (to_right, s < n_surf - 1),
        (to_left, s > 0),
    )
    receives = (
        (to_above, w > 0, from_below),
        (to_below, w < n_wall - 1, from_above),
        (to_right, s > 0, from_left),
        (to_left, s < n_surf - 1, from_right),
    )
    for copy, wanted in sends:
        pl.when(wanted)(copy.start)

    def interior(c, carry):
        for g in range(groups):
            rows = pl.ds(8 + 8 * g, 8)
            high = [field[v, c, rows, :] for v in range(NV)]
            low = [field[v, c, pl.ds(7 + 8 * g, 8), :] for v in range(NV)]
            for k, h in enumerate(face(low, high)):
                wall_h[k, c, pl.ds(8 * g, 8), :] = h
            low = [before[v, c, pl.ds(8 * g, 8), :] for v in range(NV)]
            for k, h in enumerate(face(low, high)):
                surf_h[k, c, pl.ds(8 * g, 8), :] = h
        return carry

    for v in range(NV):
        field[v, :, 0:8, :] = jnp.zeros((chunks, 8, LANES), jnp.float32)
    lax.fori_loop(0, chunks, interior, 0)
    window[...] = jnp.zeros_like(window)

    for copy, wanted, landing in receives:
        pl.when(wanted)(copy.wait_recv)

        @pl.when(jnp.logical_not(wanted))
        def _():
            landing[...] = jnp.zeros_like(landing)

    below = face([from_below[v] for v in range(NV)], [row_low[v] for v in range(NV)])
    above = face([row_high[v] for v in range(NV)], [from_above[v] for v in range(NV)])
    for k in range(3):
        for c in range(chunks):
            wall_h[k, c, 0:1, :] = below[k][c : c + 1]
            wall_h[k, c, layers : layers + 1, :] = above[k][c : c + 1]
    for g in range(groups):
        rows = pl.ds(8 * g, 8)
        left = from_left[rows, :]
        right = from_right[rows, :]
        left = [jnp.broadcast_to(left[:, v : v + 1], (8, LANES)) for v in range(NV)]
        right = [jnp.broadcast_to(right[:, v : v + 1], (8, LANES)) for v in range(NV)]
        inner = pl.ds(8 + 8 * g, 8)
        first = face(left, [field[v, 0, inner, :] for v in range(NV)])
        last = face([field[v, chunks - 1, inner, :] for v in range(NV)], right)
        for k in range(3):
            surf_h[k, 0, rows, :] = jnp.where(lane == 0, first[k], surf_h[k, 0, rows, :])
            surf_h[k, chunks, rows, :] = pltpu.roll(last[k], 1, 1)

    for load in loads[3:]:
        load.wait()

    def gather_points(c, carry):
        span = pl.ds(pl.multiple_of(c * LANES, LANES), LANES)
        sens, index, weight = [], [], []
        for g in range(groups):
            rows = pl.ds(8 * g, 8)
            live = blank_in[rows, span].astype(jnp.float32)
            index.append([index_in[t, rows, span] for t in range(2)])
            weight.append([live * weight_in[t, rows, span] for t in range(2)])
            sens.append(
                [
                    wall_h[k, c, rows, :]
                    - wall_h[k, c, pl.ds(8 * g + 1, 8), :]
                    + surf_h[k, c, rows, :]
                    - jnp.where(
                        lane == LANES - 1,
                        pltpu.roll(surf_h[k, c + 1, rows, :], LANES - 1, 1),
                        pltpu.roll(surf_h[k, c, rows, :], LANES - 1, 1),
                    )
                    for k in range(3)
                ]
            )
        sums = [[], [], []]
        for offset in range(16):
            total = [None] * 3
            for g in range(groups):
                picked = jnp.where(index[g][0] == offset, weight[g][0], 0.0) + jnp.where(
                    index[g][1] == offset, weight[g][1], 0.0
                )
                for k in range(3):
                    term = picked * sens[g][k]
                    total[k] = term if total[k] is None else total[k] + term
            for k in range(3):
                sums[k].append(total[k])
        for k in range(3):
            down = pltpu.roll(fold(sums[k][:8], sub), LANES - 8, 1, stride=1, stride_axis=0)
            up = pltpu.roll(fold(sums[k][8:], sub), 0, 1, stride=1, stride_axis=0)
            to_left = lane >= LANES - 8 + sub
            to_right = lane < sub
            window[k, c] += jnp.where(to_left, down, 0.0)
            window[k, c + 1] += jnp.where(to_left, 0.0, down) + jnp.where(to_right, 0.0, up)
            window[k, c + 2] += jnp.where(to_right, up, 0.0)
        return carry

    lax.fori_loop(0, chunks, gather_points, 0)

    points = [fold([window[k, c + 1] for c in range(chunks)], sub) for k in range(3)]
    over = [jnp.sum(window[k, 0] + window[k, chunks + 1], axis=0, keepdims=True) for k in range(3)]

    for r in range(n_surf // 8):
        local = owner_in[pl.ds(s + 8 * r * n_surf, 8, stride=n_surf), :] - s * columns
        place = local & (LANES - 1)
        chunk = local >> 7
        for k in range(3):
            value = jnp.zeros((8, LANES), jnp.float32)
            for c in range(chunks):
                row = jnp.broadcast_to(points[k][c : c + 1], (8, LANES))
                value = jnp.where(chunk == c, jnp.take_along_axis(row, place, axis=1), value)
            packet[pl.ds(64 * r + k, 8, stride=8), :] = value
            packet[pl.ds(64 * r + 3 + k, 8, stride=8), :] = jnp.broadcast_to(over[k], (8, LANES))

    me = pl.ds(pl.multiple_of((w * n_surf + s) * 8, 8), 8)
    for peer in peers:
        pltpu.make_async_remote_copy(
            src_ref=packet.at[pl.ds(pl.multiple_of(peer[1] * 8, 8), 8), :],
            dst_ref=arrived.at[me, :],
            send_sem=slot_send,
            recv_sem=slot_recv,
            device_id=peer,
            device_id_type=pl.DeviceIdType.MESH,
        ).start()
    arrived[me, :] = packet[pl.ds(pl.multiple_of(s * 8, 8), 8), :]
    for copy, wanted in sends:
        pl.when(wanted)(copy.wait_send)
    others = arrived.at[pl.ds(0, 8 * len(peers)), :]
    pltpu.make_async_copy(others, others, slot_recv).wait()

    def from_all(row, first, count):
        rows = [
            arrived[pl.ds((other * n_surf + first) * 8 + row, count, stride=8), :]
            for other in range(n_wall)
        ]
        return functools.reduce(lambda a, b: a + b, rows)

    over = [from_all(3 + k, 0, n_surf) for k in range(3)]
    for k in range(3):
        ahead = jnp.concatenate([over[k][n_surf - 1 :], over[k][: n_surf - 1]], axis=0)
        behind = jnp.concatenate([over[k][1:], over[k][:1]], axis=0)
        for r in range(n_surf // 8):
            block = sub + 8 * r
            local = owner_in[pl.ds(pl.multiple_of(s * n_surf, 8) + 8 * r, 8), :] - block * columns
            place = local & (LANES - 1)
            value = from_all(k, 8 * r, 8)
            first = jnp.take_along_axis(ahead[8 * r : 8 * r + 8], place, axis=1)
            last = jnp.take_along_axis(behind[8 * r : 8 * r + 8], place, axis=1)
            value = value + jnp.where(local < 8, first, 0.0)
            value = value + jnp.where(local >= columns - 8, last, 0.0)
            out[k, 8 * r : 8 * r + 8, :] = value
    pltpu.make_async_copy(others, others, slot_send).wait()


def body(primal, adjoint, coords, foot_index, foot_weight, blanking, owner_map):
    n_wall = lax.axis_size("wall")
    n_surf = lax.axis_size("surf")
    layers, columns = blanking.shape
    chunks = columns // LANES
    share = columns // n_surf
    owner = owner_map.reshape(n_surf * n_surf, share)
    if share < LANES:
        owner = jnp.pad(owner, ((0, 0), (0, LANES - share)))
    f32 = jnp.float32
    scratch = [
        pltpu.VMEM(primal.shape, primal.dtype),
        pltpu.VMEM(adjoint.shape, adjoint.dtype),
        pltpu.VMEM(coords.shape, coords.dtype),
        pltpu.VMEM(foot_index.shape, jnp.int32),
        pltpu.VMEM(foot_weight.shape, f32),
        pltpu.VMEM(blanking.shape, jnp.int32),
        pltpu.VMEM(owner.shape, jnp.int32),
        pltpu.VMEM((NV, chunks, layers + 8, LANES), f32),
        pltpu.VMEM((NV, chunks, layers, LANES), f32),
        pltpu.VMEM((NV, chunks, LANES), f32),
        pltpu.VMEM((NV, chunks, LANES), f32),
        pltpu.VMEM((layers, LANES), f32),
        pltpu.VMEM((layers, LANES), f32),
        pltpu.VMEM((NV, chunks, LANES), f32),
        pltpu.VMEM((NV, chunks, LANES), f32),
        pltpu.VMEM((layers, LANES), f32),
        pltpu.VMEM((layers, LANES), f32),
        pltpu.VMEM((3, chunks, layers + 8, LANES), f32),
        pltpu.VMEM((3, chunks + 1, layers, LANES), f32),
        pltpu.VMEM((3, chunks + 2, 8, LANES), f32),
        pltpu.VMEM((n_surf * 8, LANES), f32),
        pltpu.VMEM((n_wall * n_surf * 8, LANES), f32),
        pltpu.SemaphoreType.DMA((7,)),
        pltpu.SemaphoreType.DMA((4,)),
        pltpu.SemaphoreType.DMA((4,)),
        pltpu.SemaphoreType.DMA,
        pltpu.SemaphoreType.DMA,
    ]
    summed = pl.pallas_call(
        functools.partial(kernel, n_wall, n_surf),
        out_shape=jax.ShapeDtypeStruct((3, n_surf, LANES), f32),
        in_specs=[pl.BlockSpec(memory_space=pl.ANY)] * 7,
        out_specs=pl.BlockSpec(memory_space=pltpu.VMEM),
        scratch_shapes=scratch,
        compiler_params=pltpu.CompilerParams(
            collective_id=0, has_side_effects=True, vmem_limit_bytes=60 * 1024 * 1024
        ),
    )(primal, adjoint, coords, foot_index, foot_weight, blanking, owner)
    return summed[:, :, :share].reshape(3, columns)


def solution(mesh):
    placed = (
        P(None, "wall", "surf"),
        P(None, "wall", "surf"),
        P(None, "wall", "surf"),
        P(None, "wall", "surf"),
        P(None, "wall", "surf"),
        P("wall", "surf"),
        P(),
    )
    return jax.shard_map(
        body, mesh=mesh, in_specs=placed, out_specs=P(None, "surf"), check_vma=False
    )
```

```python
import functools

import jax
import jax.numpy as jnp
from jax import lax
from jax.experimental import pallas as pl
from jax.experimental.pallas import tpu as pltpu
from jax.sharding import PartitionSpec as P

LANES = 128
NV = 15


def face(low, high):
    jumps = [low[6 + v] - high[6 + v] for v in range(6)]
    sums = [low[v] + high[v] for v in range(6)]
    along = sum(jumps[v] * sums[v] for v in range(6)) * 0.25
    across = sum(jumps[v] * (high[v] - low[v]) for v in range(6))
    half = 0.5 * sums[4]
    return [
        along * sums[1 + k] + half * jumps[1 + k] - across * (high[12 + k] - low[12 + k])
        for k in range(3)
    ]


def fold(tiles, sub):
    for bit in (1, 2, 4):
        clear = (sub & bit) == 0
        folded = []
        for a, b in zip(tiles[0::2], tiles[1::2]):
            folded.append(jnp.where(clear, a, b) + pltpu.roll(jnp.where(clear, b, a), bit, 0))
        tiles = folded
    return tiles[0]


def kernel(
    n_wall,
    n_surf,
    primal,
    adjoint,
    coords,
    foot_index,
    foot_weight,
    blanking,
    owner,
    out,
    q_in,
    a_in,
    x_in,
    index_in,
    weight_in,
    blank_in,
    owner_in,
    field,
    before,
    row_low,
    row_high,
    col_low,
    col_high,
    from_below,
    from_above,
    from_left,
    from_right,
    wall_h,
    surf_h,
    window,
    packet,
    arrived,
    load_sem,
    halo_send,
    halo_recv,
    slot_send,
    slot_recv,
):
    layers, columns = blank_in.shape
    chunks = columns // LANES
    groups = layers // 8
    w = lax.axis_index("wall")
    s = lax.axis_index("surf")

    loads = [
        pltpu.make_async_copy(src, dst, load_sem.at[i])
        for i, (src, dst) in enumerate(
            (
                (primal, q_in),
                (adjoint, a_in),
                (coords, x_in),
                (foot_index, index_in),
                (foot_weight, weight_in),
                (blanking, blank_in),
                (owner, owner_in),
            )
        )
    ]
    for load in loads:
        load.start()

    barrier = pltpu.get_barrier_semaphore()
    peers = [
        (lax.rem(w + up, n_wall), lax.rem(s + along, n_surf))
        for along in range(n_surf)
        for up in range(n_wall)
        if up or along
    ]
    for peer in peers:
        pl.semaphore_signal(barrier, inc=1, device_id=peer, device_id_type=pl.DeviceIdType.MESH)

    lane32 = lax.broadcasted_iota(jnp.int32, (layers, LANES), 1)
    lane = lax.broadcasted_iota(jnp.int32, (8, LANES), 1)
    sub = lax.broadcasted_iota(jnp.int32, (8, LANES), 0)

    t_low = jnp.zeros((layers, LANES), jnp.float32)
    t_high = jnp.zeros((layers, LANES), jnp.float32)
    for v in range(NV):
        if v in (0, 6, 12):
            loads[v // 6].wait()
        source = (q_in, a_in, x_in)[v // 6]
        previous = None
        for c in range(chunks):
            x = source[v % 6, :, c * LANES : (c + 1) * LANES].astype(jnp.float32)
            field[v, c, 8 : 8 + layers, :] = x
            row_low[v, c : c + 1, :] = x[0:1]
            row_high[v, c : c + 1, :] = x[layers - 1 : layers]
            rolled = pltpu.roll(x, 1, 1)
            before[v, c] = rolled if c == 0 else jnp.where(lane32 == 0, previous, rolled)
            previous = rolled
            if c == 0:
                t_low = jnp.where(lane32 == v, jnp.broadcast_to(x[:, 0:1], x.shape), t_low)
            if c == chunks - 1:
                t_high = jnp.where(
                    lane32 == v, jnp.broadcast_to(x[:, LANES - 1 : LANES], x.shape), t_high
                )
    col_low[...] = t_low
    col_high[...] = t_high

    pl.semaphore_wait(barrier, len(peers))

    def halo(number, src, dst, target):
        return pltpu.make_async_remote_copy(
            src_ref=src,
            dst_ref=dst,
            send_sem=halo_send.at[number],
            recv_sem=halo_recv.at[number],
            device_id=target,
            device_id_type=pl.DeviceIdType.MESH,
        )

    to_above = halo(0, row_high, from_below, (lax.rem(w + 1, n_wall), s))
    to_below = halo(1, row_low, from_above, (lax.rem(w + n_wall - 1, n_wall), s))
    to_right = halo(2, col_high, from_left, (w, lax.rem(s + 1, n_surf)))
    to_left = halo(3, col_low, from_right, (w, lax.rem(s + n_surf - 1, n_surf)))
    sends = (
        (to_above, w < n_wall - 1),
        (to_below, w > 0),
        (to_right, s < n_surf - 1),
        (to_left, s > 0),
    )
    receives = (
        (to_above, w > 0, from_below),
        (to_below, w < n_wall - 1, from_above),
        (to_right, s > 0, from_left),
        (to_left, s < n_surf - 1, from_right),
    )
    for copy, wanted in sends:
        pl.when(wanted)(copy.start)

    def interior(c, carry):
        for g in range(groups):
            rows = pl.ds(8 + 8 * g, 8)
            high = [field[v, c, rows, :] for v in range(NV)]
            low = [field[v, c, pl.ds(7 + 8 * g, 8), :] for v in range(NV)]
            for k, h in enumerate(face(low, high)):
                wall_h[k, c, pl.ds(8 * g, 8), :] = h
            low = [before[v, c, pl.ds(8 * g, 8), :] for v in range(NV)]
            for k, h in enumerate(face(low, high)):
                surf_h[k, c, pl.ds(8 * g, 8), :] = h
        return carry

    for v in range(NV):
        field[v, :, 0:8, :] = jnp.zeros((chunks, 8, LANES), jnp.float32)
    lax.fori_loop(0, chunks, interior, 0, unroll=2)
    window[...] = jnp.zeros_like(window)

    for copy, wanted, landing in receives:
        pl.when(wanted)(copy.wait_recv)

        @pl.when(jnp.logical_not(wanted))
        def _():
            landing[...] = jnp.zeros_like(landing)

    below = face([from_below[v] for v in range(NV)], [row_low[v] for v in range(NV)])
    above = face([row_high[v] for v in range(NV)], [from_above[v] for v in range(NV)])
    for k in range(3):
        for c in range(chunks):
            wall_h[k, c, 0:1, :] = below[k][c : c + 1]
            wall_h[k, c, layers : layers + 1, :] = above[k][c : c + 1]
    for g in range(groups):
        rows = pl.ds(8 * g, 8)
        left = from_left[rows, :]
        right = from_right[rows, :]
        left = [jnp.broadcast_to(left[:, v : v + 1], (8, LANES)) for v in range(NV)]
        right = [jnp.broadcast_to(right[:, v : v + 1], (8, LANES)) for v in range(NV)]
        inner = pl.ds(8 + 8 * g, 8)
        first = face(left, [field[v, 0, inner, :] for v in range(NV)])
        last = face([field[v, chunks - 1, inner, :] for v in range(NV)], right)
        for k in range(3):
            surf_h[k, 0, rows, :] = jnp.where(lane == 0, first[k], surf_h[k, 0, rows, :])
            surf_h[k, chunks, rows, :] = pltpu.roll(last[k], 1, 1)

    for load in loads[3:]:
        load.wait()

    def gather_points(c, carry):
        span = pl.ds(pl.multiple_of(c * LANES, LANES), LANES)
        sens, index, weight = [], [], []
        for g in range(groups):
            rows = pl.ds(8 * g, 8)
            live = blank_in[rows, span].astype(jnp.float32)
            index.append([index_in[t, rows, span] for t in range(2)])
            weight.append([live * weight_in[t, rows, span] for t in range(2)])
            sens.append(
                [
                    wall_h[k, c, rows, :]
                    - wall_h[k, c, pl.ds(8 * g + 1, 8), :]
                    + surf_h[k, c, rows, :]
                    - jnp.where(
                        lane == LANES - 1,
                        pltpu.roll(surf_h[k, c + 1, rows, :], LANES - 1, 1),
                        pltpu.roll(surf_h[k, c, rows, :], LANES - 1, 1),
                    )
                    for k in range(3)
                ]
            )
        sums = [[], [], []]
        for offset in range(16):
            total = [None] * 3
            for g in range(groups):
                picked = jnp.where(index[g][0] == offset, weight[g][0], 0.0) + jnp.where(
                    index[g][1] == offset, weight[g][1], 0.0
                )
                for k in range(3):
                    term = picked * sens[g][k]
                    total[k] = term if total[k] is None else total[k] + term
            for k in range(3):
                sums[k].append(total[k])
        for k in range(3):
            down = pltpu.roll(fold(sums[k][:8], sub), LANES - 8, 1, stride=1, stride_axis=0)
            up = pltpu.roll(fold(sums[k][8:], sub), 0, 1, stride=1, stride_axis=0)
            to_left = lane >= LANES - 8 + sub
            to_right = lane < sub
            window[k, c] += jnp.where(to_left, down, 0.0)
            window[k, c + 1] += jnp.where(to_left, 0.0, down) + jnp.where(to_right, 0.0, up)
            window[k, c + 2] += jnp.where(to_right, up, 0.0)
        return carry

    lax.fori_loop(0, chunks, gather_points, 0, unroll=True)

    points = [fold([window[k, c + 1] for c in range(chunks)], sub) for k in range(3)]
    over = [jnp.sum(window[k, 0] + window[k, chunks + 1], axis=0, keepdims=True) for k in range(3)]

    spill = over[0] + pltpu.roll(over[1], 16, 1) + pltpu.roll(over[2], 32, 1)
    for r in range(n_surf // 8):
        local = owner_in[pl.ds(s + 8 * r * n_surf, 8, stride=n_surf), :] - s * columns
        place = local & (LANES - 1)
        chunk = local >> 7
        for k in range(3):
            value = jnp.zeros((8, LANES), jnp.float32)
            for c in range(chunks):
                row = jnp.broadcast_to(points[k][c : c + 1], (8, LANES))
                value = jnp.where(chunk == c, jnp.take_along_axis(row, place, axis=1), value)
            packet[pl.ds(64 * r + k, 8, stride=8), :] = value
        packet[pl.ds(64 * r + 3, 8, stride=8), :] = jnp.broadcast_to(spill, (8, LANES))

    me = pl.ds(pl.multiple_of((w * n_surf + s) * 8, 8), 4)
    for peer in peers:
        pltpu.make_async_remote_copy(
            src_ref=packet.at[pl.ds(pl.multiple_of(peer[1] * 8, 8), 4), :],
            dst_ref=arrived.at[me, :],
            send_sem=slot_send,
            recv_sem=slot_recv,
            device_id=peer,
            device_id_type=pl.DeviceIdType.MESH,
        ).start()
    arrived[me, :] = packet[pl.ds(pl.multiple_of(s * 8, 8), 4), :]
    for copy, wanted in sends:
        pl.when(wanted)(copy.wait_send)
    others = arrived.at[pl.ds(0, 4 * len(peers)), :]
    pltpu.make_async_copy(others, others, slot_recv).wait()

    def from_all(row, first, count):
        rows = [
            arrived[pl.ds((other * n_surf + first) * 8 + row, count, stride=8), :]
            for other in range(n_wall)
        ]
        return functools.reduce(lambda a, b: a + b, rows)

    spill = from_all(3, 0, n_surf)
    ahead = jnp.concatenate([spill[n_surf - 1 :], spill[: n_surf - 1]], axis=0)
    behind = jnp.concatenate([spill[1:], spill[:1]], axis=0)
    for k in range(3):
        for r in range(n_surf // 8):
            block = sub + 8 * r
            local = owner_in[pl.ds(pl.multiple_of(s * n_surf, 8) + 8 * r, 8), :] - block * columns
            place = (local + 16 * k) & (LANES - 1)
            value = from_all(k, 8 * r, 8)
            first = jnp.take_along_axis(ahead[8 * r : 8 * r + 8], place, axis=1)
            last = jnp.take_along_axis(behind[8 * r : 8 * r + 8], place, axis=1)
            value = value + jnp.where(local < 8, first, 0.0)
            value = value + jnp.where(local >= columns - 8, last, 0.0)
            out[k, 8 * r : 8 * r + 8, :] = value
    pltpu.make_async_copy(others, others, slot_send).wait()


def body(primal, adjoint, coords, foot_index, foot_weight, blanking, owner_map):
    n_wall = lax.axis_size("wall")
    n_surf = lax.axis_size("surf")
    layers, columns = blanking.shape
    chunks = columns // LANES
    share = columns // n_surf
    owner = owner_map.reshape(n_surf * n_surf, share)
    if share < LANES:
        owner = jnp.pad(owner, ((0, 0), (0, LANES - share)))
    f32 = jnp.float32
    scratch = [
        pltpu.VMEM(primal.shape, primal.dtype),
        pltpu.VMEM(adjoint.shape, adjoint.dtype),
        pltpu.VMEM(coords.shape, coords.dtype),
        pltpu.VMEM(foot_index.shape, jnp.int32),
        pltpu.VMEM(foot_weight.shape, f32),
        pltpu.VMEM(blanking.shape, jnp.int32),
        pltpu.VMEM(owner.shape, jnp.int32),
        pltpu.VMEM((NV, chunks, layers + 8, LANES), f32),
        pltpu.VMEM((NV, chunks, layers, LANES), f32),
        pltpu.VMEM((NV, chunks, LANES), f32),
        pltpu.VMEM((NV, chunks, LANES), f32),
        pltpu.VMEM((layers, LANES), f32),
        pltpu.VMEM((layers, LANES), f32),
        pltpu.VMEM((NV, chunks, LANES), f32),
        pltpu.VMEM((NV, chunks, LANES), f32),
        pltpu.VMEM((layers, LANES), f32),
        pltpu.VMEM((layers, LANES), f32),
        pltpu.VMEM((3, chunks, layers + 8, LANES), f32),
        pltpu.VMEM((3, chunks + 1, layers, LANES), f32),
        pltpu.VMEM((3, chunks + 2, 8, LANES), f32),
        pltpu.VMEM((n_surf * 8, LANES), f32),
        pltpu.VMEM((n_wall * n_surf * 8, LANES), f32),
        pltpu.SemaphoreType.DMA((7,)),
        pltpu.SemaphoreType.DMA((4,)),
        pltpu.SemaphoreType.DMA((4,)),
        pltpu.SemaphoreType.DMA,
        pltpu.SemaphoreType.DMA,
    ]
    summed = pl.pallas_call(
        functools.partial(kernel, n_wall, n_surf),
        out_shape=jax.ShapeDtypeStruct((3, n_surf, LANES), f32),
        in_specs=[pl.BlockSpec(memory_space=pl.ANY)] * 7,
        out_specs=pl.BlockSpec(memory_space=pltpu.VMEM),
        scratch_shapes=scratch,
        compiler_params=pltpu.CompilerParams(
            collective_id=0, has_side_effects=True, vmem_limit_bytes=60 * 1024 * 1024
        ),
    )(primal, adjoint, coords, foot_index, foot_weight, blanking, owner)
    return summed[:, :, :share].reshape(3, columns)


def solution(mesh):
    placed = (
        P(None, "wall", "surf"),
        P(None, "wall", "surf"),
        P(None, "wall", "surf"),
        P(None, "wall", "surf"),
        P(None, "wall", "surf"),
        P("wall", "surf"),
        P(),
    )
    return jax.shard_map(
        body, mesh=mesh, in_specs=placed, out_specs=P(None, "surf"), check_vma=False
    )
```

```python
import functools

import jax
import jax.numpy as jnp
from jax import lax
from jax.experimental import pallas as pl
from jax.experimental.pallas import tpu as pltpu
from jax.sharding import PartitionSpec as P

LANES = 128
NV = 15


def face(low, high):
    jumps = [low[6 + v] - high[6 + v] for v in range(6)]
    sums = [low[v] + high[v] for v in range(6)]
    along = sum(jumps[v] * sums[v] for v in range(6)) * 0.25
    across = sum(jumps[v] * (high[v] - low[v]) for v in range(6))
    half = 0.5 * sums[4]
    return [
        along * sums[1 + k] + half * jumps[1 + k] - across * (high[12 + k] - low[12 + k])
        for k in range(3)
    ]


def fold(tiles, sub):
    for bit in (1, 2, 4):
        clear = (sub & bit) == 0
        folded = []
        for a, b in zip(tiles[0::2], tiles[1::2]):
            folded.append(jnp.where(clear, a, b) + pltpu.roll(jnp.where(clear, b, a), bit, 0))
        tiles = folded
    return tiles[0]


def kernel(
    n_wall,
    n_surf,
    primal,
    adjoint,
    coords,
    foot_index,
    foot_weight,
    blanking,
    owner,
    out,
    q_in,
    a_in,
    x_in,
    index_in,
    weight_in,
    blank_in,
    owner_in,
    field,
    before,
    row_low,
    row_high,
    col_low,
    col_high,
    from_below,
    from_above,
    from_left,
    from_right,
    wall_h,
    surf_h,
    window,
    packet,
    arrived,
    load_sem,
    halo_send,
    halo_recv,
    slot_send,
    slot_recv,
):
    layers, columns = blank_in.shape
    chunks = columns // LANES
    groups = layers // 8
    w = lax.axis_index("wall")
    s = lax.axis_index("surf")

    loads = [
        pltpu.make_async_copy(src, dst, load_sem.at[i])
        for i, (src, dst) in enumerate(
            (
                (primal, q_in),
                (adjoint, a_in),
                (coords, x_in),
                (foot_index, index_in),
                (foot_weight, weight_in),
                (blanking, blank_in),
                (owner, owner_in),
            )
        )
    ]
    for load in loads:
        load.start()

    barrier = pltpu.get_barrier_semaphore()
    peers = [
        (lax.rem(w + up, n_wall), lax.rem(s + along, n_surf))
        for along in range(n_surf)
        for up in range(n_wall)
        if up or along
    ]
    for peer in peers:
        pl.semaphore_signal(barrier, inc=1, device_id=peer, device_id_type=pl.DeviceIdType.MESH)

    lane32 = lax.broadcasted_iota(jnp.int32, (layers, LANES), 1)
    lane = lax.broadcasted_iota(jnp.int32, (8, LANES), 1)
    sub = lax.broadcasted_iota(jnp.int32, (8, LANES), 0)

    t_low = jnp.zeros((layers, LANES), jnp.float32)
    t_high = jnp.zeros((layers, LANES), jnp.float32)
    for v in range(NV):
        if v in (0, 6, 12):
            loads[v // 6].wait()
        source = (q_in, a_in, x_in)[v // 6]
        previous = None
        for c in range(chunks):
            x = source[v % 6, :, c * LANES : (c + 1) * LANES].astype(jnp.float32)
            field[v, c, 8 : 8 + layers, :] = x
            row_low[v, c : c + 1, :] = x[0:1]
            row_high[v, c : c + 1, :] = x[layers - 1 : layers]
            rolled = pltpu.roll(x, 1, 1)
            before[v, c] = rolled if c == 0 else jnp.where(lane32 == 0, previous, rolled)
            previous = rolled
            if c == 0:
                t_low = jnp.where(lane32 == v, jnp.broadcast_to(x[:, 0:1], x.shape), t_low)
            if c == chunks - 1:
                t_high = jnp.where(
                    lane32 == v, jnp.broadcast_to(x[:, LANES - 1 : LANES], x.shape), t_high
                )
    col_low[...] = t_low
    col_high[...] = t_high

    pl.semaphore_wait(barrier, len(peers))

    def halo(number, src, dst, target):
        return pltpu.make_async_remote_copy(
            src_ref=src,
            dst_ref=dst,
            send_sem=halo_send.at[number],
            recv_sem=halo_recv.at[number],
            device_id=target,
            device_id_type=pl.DeviceIdType.MESH,
        )

    to_above = halo(0, row_high, from_below, (lax.rem(w + 1, n_wall), s))
    to_below = halo(1, row_low, from_above, (lax.rem(w + n_wall - 1, n_wall), s))
    to_right = halo(2, col_high, from_left, (w, lax.rem(s + 1, n_surf)))
    to_left = halo(3, col_low, from_right, (w, lax.rem(s + n_surf - 1, n_surf)))
    sends = (
        (to_above, w < n_wall - 1),
        (to_below, w > 0),
        (to_right, s < n_surf - 1),
        (to_left, s > 0),
    )
    receives = (
        (to_above, w > 0, from_below),
        (to_below, w < n_wall - 1, from_above),
        (to_right, s > 0, from_left),
        (to_left, s < n_surf - 1, from_right),
    )
    for copy, wanted in sends:
        pl.when(wanted)(copy.start)

    def interior(c, carry):
        for g in range(groups):
            rows = pl.ds(8 + 8 * g, 8)
            high = [field[v, c, rows, :] for v in range(NV)]
            low = [field[v, c, pl.ds(7 + 8 * g, 8), :] for v in range(NV)]
            for k, h in enumerate(face(low, high)):
                wall_h[k, c, pl.ds(8 * g, 8), :] = h
            low = [before[v, c, pl.ds(8 * g, 8), :] for v in range(NV)]
            for k, h in enumerate(face(low, high)):
                surf_h[k, c, pl.ds(8 * g, 8), :] = h
        return carry

    for v in range(NV):
        field[v, :, 0:8, :] = jnp.zeros((chunks, 8, LANES), jnp.float32)
    lax.fori_loop(0, chunks, interior, 0, unroll=2)
    window[...] = jnp.zeros_like(window)
    for load in loads[3:]:
        load.wait()

    def gather_points(c, chosen):
        span = pl.ds(c * LANES, LANES)
        sens, index, weight = [], [], []
        for g in chosen:
            rows = pl.ds(8 * g, 8)
            live = blank_in[rows, span].astype(jnp.float32)
            index.append([index_in[t, rows, span] for t in range(2)])
            weight.append([live * weight_in[t, rows, span] for t in range(2)])
            sens.append(
                [
                    wall_h[k, c, rows, :]
                    - wall_h[k, c, pl.ds(8 * g + 1, 8), :]
                    + surf_h[k, c, rows, :]
                    - jnp.where(
                        lane == LANES - 1,
                        pltpu.roll(surf_h[k, c + 1, rows, :], LANES - 1, 1),
                        pltpu.roll(surf_h[k, c, rows, :], LANES - 1, 1),
                    )
                    for k in range(3)
                ]
            )
        sums = [[], [], []]
        for offset in range(16):
            total = [None] * 3
            for g in range(len(chosen)):
                picked = jnp.where(index[g][0] == offset, weight[g][0], 0.0) + jnp.where(
                    index[g][1] == offset, weight[g][1], 0.0
                )
                for k in range(3):
                    term = picked * sens[g][k]
                    total[k] = term if total[k] is None else total[k] + term
            for k in range(3):
                sums[k].append(total[k])
        for k in range(3):
            down = pltpu.roll(fold(sums[k][:8], sub), LANES - 8, 1, stride=1, stride_axis=0)
            up = pltpu.roll(fold(sums[k][8:], sub), 0, 1, stride=1, stride_axis=0)
            to_left = lane >= LANES - 8 + sub
            to_right = lane < sub
            window[k, c] += jnp.where(to_left, down, 0.0)
            window[k, c + 1] += jnp.where(to_left, 0.0, down) + jnp.where(to_right, 0.0, up)
            window[k, c + 2] += jnp.where(to_right, up, 0.0)

    for c in range(1, chunks - 1):
        gather_points(c, range(1, groups - 1))


    for copy, wanted, landing in receives:
        pl.when(wanted)(copy.wait_recv)

        @pl.when(jnp.logical_not(wanted))
        def _():
            landing[...] = jnp.zeros_like(landing)

    below = face([from_below[v] for v in range(NV)], [row_low[v] for v in range(NV)])
    above = face([row_high[v] for v in range(NV)], [from_above[v] for v in range(NV)])
    for k in range(3):
        for c in range(chunks):
            wall_h[k, c, 0:1, :] = below[k][c : c + 1]
            wall_h[k, c, layers : layers + 1, :] = above[k][c : c + 1]
    for g in range(groups):
        rows = pl.ds(8 * g, 8)
        left = from_left[rows, :]
        right = from_right[rows, :]
        left = [jnp.broadcast_to(left[:, v : v + 1], (8, LANES)) for v in range(NV)]
        right = [jnp.broadcast_to(right[:, v : v + 1], (8, LANES)) for v in range(NV)]
        inner = pl.ds(8 + 8 * g, 8)
        first = face(left, [field[v, 0, inner, :] for v in range(NV)])
        last = face([field[v, chunks - 1, inner, :] for v in range(NV)], right)
        for k in range(3):
            surf_h[k, 0, rows, :] = jnp.where(lane == 0, first[k], surf_h[k, 0, rows, :])
            surf_h[k, chunks, rows, :] = pltpu.roll(last[k], 1, 1)

    for c in range(chunks):
        edge = c in (0, chunks - 1)
        gather_points(c, range(groups) if edge else (0, groups - 1))

    points = [fold([window[k, c + 1] for c in range(chunks)], sub) for k in range(3)]
    over = [jnp.sum(window[k, 0] + window[k, chunks + 1], axis=0, keepdims=True) for k in range(3)]

    spill = over[0] + pltpu.roll(over[1], 16, 1) + pltpu.roll(over[2], 32, 1)
    for r in range(n_surf // 8):
        local = owner_in[pl.ds(s + 8 * r * n_surf, 8, stride=n_surf), :] - s * columns
        place = local & (LANES - 1)
        chunk = local >> 7
        for k in range(3):
            value = jnp.zeros((8, LANES), jnp.float32)
            for c in range(chunks):
                row = jnp.broadcast_to(points[k][c : c + 1], (8, LANES))
                value = jnp.where(chunk == c, jnp.take_along_axis(row, place, axis=1), value)
            packet[pl.ds(64 * r + k, 8, stride=8), :] = value
        packet[pl.ds(64 * r + 3, 8, stride=8), :] = jnp.broadcast_to(spill, (8, LANES))

    me = pl.ds(pl.multiple_of((w * n_surf + s) * 8, 8), 4)
    for peer in peers:
        pltpu.make_async_remote_copy(
            src_ref=packet.at[pl.ds(pl.multiple_of(peer[1] * 8, 8), 4), :],
            dst_ref=arrived.at[me, :],
            send_sem=slot_send,
            recv_sem=slot_recv,
            device_id=peer,
            device_id_type=pl.DeviceIdType.MESH,
        ).start()
    arrived[me, :] = packet[pl.ds(pl.multiple_of(s * 8, 8), 4), :]
    for copy, wanted in sends:
        pl.when(wanted)(copy.wait_send)
    others = arrived.at[pl.ds(0, 4 * len(peers)), :]
    pltpu.make_async_copy(others, others, slot_recv).wait()

    def from_all(row, first, count):
        rows = [
            arrived[pl.ds((other * n_surf + first) * 8 + row, count, stride=8), :]
            for other in range(n_wall)
        ]
        return functools.reduce(lambda a, b: a + b, rows)

    spill = from_all(3, 0, n_surf)
    ahead = jnp.concatenate([spill[n_surf - 1 :], spill[: n_surf - 1]], axis=0)
    behind = jnp.concatenate([spill[1:], spill[:1]], axis=0)
    for k in range(3):
        for r in range(n_surf // 8):
            block = sub + 8 * r
            local = owner_in[pl.ds(pl.multiple_of(s * n_surf, 8) + 8 * r, 8), :] - block * columns
            place = (local + 16 * k) & (LANES - 1)
            value = from_all(k, 8 * r, 8)
            first = jnp.take_along_axis(ahead[8 * r : 8 * r + 8], place, axis=1)
            last = jnp.take_along_axis(behind[8 * r : 8 * r + 8], place, axis=1)
            value = value + jnp.where(local < 8, first, 0.0)
            value = value + jnp.where(local >= columns - 8, last, 0.0)
            out[k, 8 * r : 8 * r + 8, :] = value
    pltpu.make_async_copy(others, others, slot_send).wait()


def body(primal, adjoint, coords, foot_index, foot_weight, blanking, owner_map):
    n_wall = lax.axis_size("wall")
    n_surf = lax.axis_size("surf")
    layers, columns = blanking.shape
    chunks = columns // LANES
    share = columns // n_surf
    owner = owner_map.reshape(n_surf * n_surf, share)
    if share < LANES:
        owner = jnp.pad(owner, ((0, 0), (0, LANES - share)))
    f32 = jnp.float32
    scratch = [
        pltpu.VMEM(primal.shape, primal.dtype),
        pltpu.VMEM(adjoint.shape, adjoint.dtype),
        pltpu.VMEM(coords.shape, coords.dtype),
        pltpu.VMEM(foot_index.shape, jnp.int32),
        pltpu.VMEM(foot_weight.shape, f32),
        pltpu.VMEM(blanking.shape, jnp.int32),
        pltpu.VMEM(owner.shape, jnp.int32),
        pltpu.VMEM((NV, chunks, layers + 8, LANES), f32),
        pltpu.VMEM((NV, chunks, layers, LANES), f32),
        pltpu.VMEM((NV, chunks, LANES), f32),
        pltpu.VMEM((NV, chunks, LANES), f32),
        pltpu.VMEM((layers, LANES), f32),
        pltpu.VMEM((layers, LANES), f32),
        pltpu.VMEM((NV, chunks, LANES), f32),
        pltpu.VMEM((NV, chunks, LANES), f32),
        pltpu.VMEM((layers, LANES), f32),
        pltpu.VMEM((layers, LANES), f32),
        pltpu.VMEM((3, chunks, layers + 8, LANES), f32),
        pltpu.VMEM((3, chunks + 1, layers, LANES), f32),
        pltpu.VMEM((3, chunks + 2, 8, LANES), f32),
        pltpu.VMEM((n_surf * 8, LANES), f32),
        pltpu.VMEM((n_wall * n_surf * 8, LANES), f32),
        pltpu.SemaphoreType.DMA((7,)),
        pltpu.SemaphoreType.DMA((4,)),
        pltpu.SemaphoreType.DMA((4,)),
        pltpu.SemaphoreType.DMA,
        pltpu.SemaphoreType.DMA,
    ]
    summed = pl.pallas_call(
        functools.partial(kernel, n_wall, n_surf),
        out_shape=jax.ShapeDtypeStruct((3, n_surf, LANES), f32),
        in_specs=[pl.BlockSpec(memory_space=pl.ANY)] * 7,
        out_specs=pl.BlockSpec(memory_space=pltpu.VMEM),
        scratch_shapes=scratch,
        compiler_params=pltpu.CompilerParams(
            collective_id=0, has_side_effects=True, vmem_limit_bytes=60 * 1024 * 1024
        ),
    )(primal, adjoint, coords, foot_index, foot_weight, blanking, owner)
    return summed[:, :, :share].reshape(3, columns)


def solution(mesh):
    placed = (
        P(None, "wall", "surf"),
        P(None, "wall", "surf"),
        P(None, "wall", "surf"),
        P(None, "wall", "surf"),
        P(None, "wall", "surf"),
        P("wall", "surf"),
        P(),
    )
    return jax.shard_map(
        body, mesh=mesh, in_specs=placed, out_specs=P(None, "surf"), check_vma=False
    )
```

```python
import functools

import jax
import jax.numpy as jnp
from jax import lax
from jax.experimental import pallas as pl
from jax.experimental.pallas import tpu as pltpu
from jax.sharding import PartitionSpec as P

LANES = 128
NV = 15


def face(low, high):
    jumps = [low[6 + v] - high[6 + v] for v in range(6)]
    sums = [low[v] + high[v] for v in range(6)]
    along = sum(jumps[v] * sums[v] for v in range(6)) * 0.25
    across = sum(jumps[v] * (high[v] - low[v]) for v in range(6))
    half = 0.5 * sums[4]
    return [
        along * sums[1 + k] + half * jumps[1 + k] - across * (high[12 + k] - low[12 + k])
        for k in range(3)
    ]


def fold(tiles, sub):
    for bit in (1, 2, 4):
        clear = (sub & bit) == 0
        folded = []
        for a, b in zip(tiles[0::2], tiles[1::2]):
            folded.append(jnp.where(clear, a, b) + pltpu.roll(jnp.where(clear, b, a), bit, 0))
        tiles = folded
    return tiles[0]


def kernel(
    n_wall,
    n_surf,
    primal,
    adjoint,
    coords,
    foot_index,
    foot_weight,
    blanking,
    owner,
    out,
    q_in,
    a_in,
    x_in,
    index_in,
    weight_in,
    blank_in,
    owner_in,
    field,
    before,
    row_low,
    row_high,
    col_low,
    col_high,
    from_below,
    from_above,
    from_left,
    from_right,
    wall_h,
    surf_h,
    window,
    packet,
    arrived,
    load_sem,
    halo_send,
    halo_recv,
    slot_send,
    slot_recv,
):
    layers, columns = blank_in.shape
    chunks = columns // LANES
    groups = layers // 8
    w = lax.axis_index("wall")
    s = lax.axis_index("surf")

    loads = [
        pltpu.make_async_copy(src, dst, load_sem.at[i])
        for i, (src, dst) in enumerate(
            (
                (primal, q_in),
                (adjoint, a_in),
                (coords, x_in),
                (foot_index, index_in),
                (foot_weight, weight_in),
                (blanking, blank_in),
                (owner, owner_in),
            )
        )
    ]
    for load in loads[:3]:
        load.start()

    barrier = pltpu.get_barrier_semaphore()
    peers = [
        (lax.rem(w + up, n_wall), lax.rem(s + along, n_surf))
        for along in range(n_surf)
        for up in range(n_wall)
        if up or along
    ]
    for peer in peers:
        pl.semaphore_signal(barrier, inc=1, device_id=peer, device_id_type=pl.DeviceIdType.MESH)

    for load in loads[3:]:
        load.start()

    lane32 = lax.broadcasted_iota(jnp.int32, (layers, LANES), 1)
    lane = lax.broadcasted_iota(jnp.int32, (8, LANES), 1)
    sub = lax.broadcasted_iota(jnp.int32, (8, LANES), 0)

    t_low = jnp.zeros((layers, LANES), jnp.float32)
    t_high = jnp.zeros((layers, LANES), jnp.float32)
    for v in range(NV):
        if v in (0, 6, 12):
            loads[v // 6].wait()
        source = (q_in, a_in, x_in)[v // 6]
        bottom = source[v % 6, 0:16, :].astype(jnp.float32)
        top = source[v % 6, layers - 16 : layers, :].astype(jnp.float32)
        for c in range(chunks):
            span = slice(c * LANES, (c + 1) * LANES)
            row_low[v, c : c + 1, :] = bottom[0:1, span]
            row_high[v, c : c + 1, :] = top[15:16, span]
        x = source[v % 6, :, 0:LANES].astype(jnp.float32)
        t_low = jnp.where(lane32 == v, jnp.broadcast_to(x[:, 0:1], x.shape), t_low)
        x = source[v % 6, :, columns - LANES : columns].astype(jnp.float32)
        t_high = jnp.where(lane32 == v, jnp.broadcast_to(x[:, LANES - 1 : LANES], x.shape), t_high)
    col_low[...] = t_low
    col_high[...] = t_high

    pl.semaphore_wait(barrier, len(peers))

    def halo(number, src, dst, target):
        return pltpu.make_async_remote_copy(
            src_ref=src,
            dst_ref=dst,
            send_sem=halo_send.at[number],
            recv_sem=halo_recv.at[number],
            device_id=target,
            device_id_type=pl.DeviceIdType.MESH,
        )

    to_above = halo(0, row_high, from_below, (lax.rem(w + 1, n_wall), s))
    to_below = halo(1, row_low, from_above, (lax.rem(w + n_wall - 1, n_wall), s))
    to_right = halo(2, col_high, from_left, (w, lax.rem(s + 1, n_surf)))
    to_left = halo(3, col_low, from_right, (w, lax.rem(s + n_surf - 1, n_surf)))
    sends = (
        (to_above, w < n_wall - 1),
        (to_below, w > 0),
        (to_right, s < n_surf - 1),
        (to_left, s > 0),
    )
    receives = (
        (to_above, w > 0, from_below),
        (to_below, w < n_wall - 1, from_above),
        (to_right, s > 0, from_left),
        (to_left, s < n_surf - 1, from_right),
    )
    for copy, wanted in sends:
        pl.when(wanted)(copy.start)

    def interior(c, carry):
        for g in range(groups):
            rows = pl.ds(8 + 8 * g, 8)
            high = [field[v, c, rows, :] for v in range(NV)]
            low = [field[v, c, pl.ds(7 + 8 * g, 8), :] for v in range(NV)]
            for k, h in enumerate(face(low, high)):
                wall_h[k, c, pl.ds(8 * g, 8), :] = h
            low = [before[v, c, pl.ds(8 * g, 8), :] for v in range(NV)]
            for k, h in enumerate(face(low, high)):
                surf_h[k, c, pl.ds(8 * g, 8), :] = h
        return carry

    for v in range(NV):
        source = (q_in, a_in, x_in)[v // 6]
        previous = None
        for c in range(chunks):
            x = source[v % 6, :, c * LANES : (c + 1) * LANES].astype(jnp.float32)
            field[v, c, 8 : 8 + layers, :] = x
            rolled = pltpu.roll(x, 1, 1)
            before[v, c] = rolled if c == 0 else jnp.where(lane32 == 0, previous, rolled)
            previous = rolled
        field[v, :, 0:8, :] = jnp.zeros((chunks, 8, LANES), jnp.float32)
    lax.fori_loop(0, chunks, interior, 0, unroll=2)
    window[...] = jnp.zeros_like(window)
    for load in loads[3:]:
        load.wait()

    def gather_points(c, chosen):
        span = pl.ds(c * LANES, LANES)
        sens, index, weight = [], [], []
        for g in chosen:
            rows = pl.ds(8 * g, 8)
            live = blank_in[rows, span].astype(jnp.float32)
            index.append([index_in[t, rows, span] for t in range(2)])
            weight.append([live * weight_in[t, rows, span] for t in range(2)])
            sens.append(
                [
                    wall_h[k, c, rows, :]
                    - wall_h[k, c, pl.ds(8 * g + 1, 8), :]
                    + surf_h[k, c, rows, :]
                    - jnp.where(
                        lane == LANES - 1,
                        pltpu.roll(surf_h[k, c + 1, rows, :], LANES - 1, 1),
                        pltpu.roll(surf_h[k, c, rows, :], LANES - 1, 1),
                    )
                    for k in range(3)
                ]
            )
        sums = [[], [], []]
        for offset in range(16):
            total = [None] * 3
            for g in range(len(chosen)):
                picked = jnp.where(index[g][0] == offset, weight[g][0], 0.0) + jnp.where(
                    index[g][1] == offset, weight[g][1], 0.0
                )
                for k in range(3):
                    term = picked * sens[g][k]
                    total[k] = term if total[k] is None else total[k] + term
            for k in range(3):
                sums[k].append(total[k])
        for k in range(3):
            down = pltpu.roll(fold(sums[k][:8], sub), LANES - 8, 1, stride=1, stride_axis=0)
            up = pltpu.roll(fold(sums[k][8:], sub), 0, 1, stride=1, stride_axis=0)
            to_left = lane >= LANES - 8 + sub
            to_right = lane < sub
            window[k, c] += jnp.where(to_left, down, 0.0)
            window[k, c + 1] += jnp.where(to_left, 0.0, down) + jnp.where(to_right, 0.0, up)
            window[k, c + 2] += jnp.where(to_right, up, 0.0)

    for c in range(1, chunks - 1):
        gather_points(c, range(1, groups - 1))


    for copy, wanted, landing in receives:
        pl.when(wanted)(copy.wait_recv)

        @pl.when(jnp.logical_not(wanted))
        def _():
            landing[...] = jnp.zeros_like(landing)

    below = face([from_below[v] for v in range(NV)], [row_low[v] for v in range(NV)])
    above = face([row_high[v] for v in range(NV)], [from_above[v] for v in range(NV)])
    for k in range(3):
        for c in range(chunks):
            wall_h[k, c, 0:1, :] = below[k][c : c + 1]
            wall_h[k, c, layers : layers + 1, :] = above[k][c : c + 1]
    for g in range(groups):
        rows = pl.ds(8 * g, 8)
        left = from_left[rows, :]
        right = from_right[rows, :]
        left = [jnp.broadcast_to(left[:, v : v + 1], (8, LANES)) for v in range(NV)]
        right = [jnp.broadcast_to(right[:, v : v + 1], (8, LANES)) for v in range(NV)]
        inner = pl.ds(8 + 8 * g, 8)
        first = face(left, [field[v, 0, inner, :] for v in range(NV)])
        last = face([field[v, chunks - 1, inner, :] for v in range(NV)], right)
        for k in range(3):
            surf_h[k, 0, rows, :] = jnp.where(lane == 0, first[k], surf_h[k, 0, rows, :])
            surf_h[k, chunks, rows, :] = pltpu.roll(last[k], 1, 1)

    for c in range(chunks):
        edge = c in (0, chunks - 1)
        gather_points(c, range(groups) if edge else (0, groups - 1))

    points = [fold([window[k, c + 1] for c in range(chunks)], sub) for k in range(3)]
    over = [jnp.sum(window[k, 0] + window[k, chunks + 1], axis=0, keepdims=True) for k in range(3)]

    spill = over[0] + pltpu.roll(over[1], 16, 1) + pltpu.roll(over[2], 32, 1)
    for r in range(n_surf // 8):
        local = owner_in[pl.ds(s + 8 * r * n_surf, 8, stride=n_surf), :] - s * columns
        place = local & (LANES - 1)
        chunk = local >> 7
        for k in range(3):
            value = jnp.zeros((8, LANES), jnp.float32)
            for c in range(chunks):
                row = jnp.broadcast_to(points[k][c : c + 1], (8, LANES))
                value = jnp.where(chunk == c, jnp.take_along_axis(row, place, axis=1), value)
            packet[pl.ds(64 * r + k, 8, stride=8), :] = value
        packet[pl.ds(64 * r + 3, 8, stride=8), :] = jnp.broadcast_to(spill, (8, LANES))

    me = pl.ds(pl.multiple_of((w * n_surf + s) * 8, 8), 4)
    for peer in peers:
        pltpu.make_async_remote_copy(
            src_ref=packet.at[pl.ds(pl.multiple_of(peer[1] * 8, 8), 4), :],
            dst_ref=arrived.at[me, :],
            send_sem=slot_send,
            recv_sem=slot_recv,
            device_id=peer,
            device_id_type=pl.DeviceIdType.MESH,
        ).start()
    arrived[me, :] = packet[pl.ds(pl.multiple_of(s * 8, 8), 4), :]
    for copy, wanted in sends:
        pl.when(wanted)(copy.wait_send)
    others = arrived.at[pl.ds(0, 4 * len(peers)), :]
    pltpu.make_async_copy(others, others, slot_recv).wait()

    def from_all(row, first, count):
        rows = [
            arrived[pl.ds((other * n_surf + first) * 8 + row, count, stride=8), :]
            for other in range(n_wall)
        ]
        return functools.reduce(lambda a, b: a + b, rows)

    spill = from_all(3, 0, n_surf)
    ahead = jnp.concatenate([spill[n_surf - 1 :], spill[: n_surf - 1]], axis=0)
    behind = jnp.concatenate([spill[1:], spill[:1]], axis=0)
    for k in range(3):
        for r in range(n_surf // 8):
            block = sub + 8 * r
            local = owner_in[pl.ds(pl.multiple_of(s * n_surf, 8) + 8 * r, 8), :] - block * columns
            place = (local + 16 * k) & (LANES - 1)
            value = from_all(k, 8 * r, 8)
            first = jnp.take_along_axis(ahead[8 * r : 8 * r + 8], place, axis=1)
            last = jnp.take_along_axis(behind[8 * r : 8 * r + 8], place, axis=1)
            value = value + jnp.where(local < 8, first, 0.0)
            value = value + jnp.where(local >= columns - 8, last, 0.0)
            out[k, 8 * r : 8 * r + 8, :] = value
    pltpu.make_async_copy(others, others, slot_send).wait()


def body(primal, adjoint, coords, foot_index, foot_weight, blanking, owner_map):
    n_wall = lax.axis_size("wall")
    n_surf = lax.axis_size("surf")
    layers, columns = blanking.shape
    chunks = columns // LANES
    share = columns // n_surf
    owner = owner_map.reshape(n_surf * n_surf, share)
    if share < LANES:
        owner = jnp.pad(owner, ((0, 0), (0, LANES - share)))
    f32 = jnp.float32
    scratch = [
        pltpu.VMEM(primal.shape, primal.dtype),
        pltpu.VMEM(adjoint.shape, adjoint.dtype),
        pltpu.VMEM(coords.shape, coords.dtype),
        pltpu.VMEM(foot_index.shape, jnp.int32),
        pltpu.VMEM(foot_weight.shape, f32),
        pltpu.VMEM(blanking.shape, jnp.int32),
        pltpu.VMEM(owner.shape, jnp.int32),
        pltpu.VMEM((NV, chunks, layers + 8, LANES), f32),
        pltpu.VMEM((NV, chunks, layers, LANES), f32),
        pltpu.VMEM((NV, chunks, LANES), f32),
        pltpu.VMEM((NV, chunks, LANES), f32),
        pltpu.VMEM((layers, LANES), f32),
        pltpu.VMEM((layers, LANES), f32),
        pltpu.VMEM((NV, chunks, LANES), f32),
        pltpu.VMEM((NV, chunks, LANES), f32),
        pltpu.VMEM((layers, LANES), f32),
        pltpu.VMEM((layers, LANES), f32),
        pltpu.VMEM((3, chunks, layers + 8, LANES), f32),
        pltpu.VMEM((3, chunks + 1, layers, LANES), f32),
        pltpu.VMEM((3, chunks + 2, 8, LANES), f32),
        pltpu.VMEM((n_surf * 8, LANES), f32),
        pltpu.VMEM((n_wall * n_surf * 8, LANES), f32),
        pltpu.SemaphoreType.DMA((7,)),
        pltpu.SemaphoreType.DMA((4,)),
        pltpu.SemaphoreType.DMA((4,)),
        pltpu.SemaphoreType.DMA,
        pltpu.SemaphoreType.DMA,
    ]
    summed = pl.pallas_call(
        functools.partial(kernel, n_wall, n_surf),
        out_shape=jax.ShapeDtypeStruct((3, n_surf, LANES), f32),
        in_specs=[pl.BlockSpec(memory_space=pl.ANY)] * 7,
        out_specs=pl.BlockSpec(memory_space=pltpu.VMEM),
        scratch_shapes=scratch,
        compiler_params=pltpu.CompilerParams(
            collective_id=0, has_side_effects=True, vmem_limit_bytes=60 * 1024 * 1024
        ),
    )(primal, adjoint, coords, foot_index, foot_weight, blanking, owner)
    return summed[:, :, :share].reshape(3, columns)


def solution(mesh):
    placed = (
        P(None, "wall", "surf"),
        P(None, "wall", "surf"),
        P(None, "wall", "surf"),
        P(None, "wall", "surf"),
        P(None, "wall", "surf"),
        P("wall", "surf"),
        P(),
    )
    return jax.shard_map(
        body, mesh=mesh, in_specs=placed, out_specs=P(None, "surf"), check_vma=False
    )
```
